256 devices in a mesh: pool: 32 (over y, x, core), tp: 8 (over z).
Axes of the slice: x: 4, y: 4, z: 8, core: 2. Of those that a mesh axis runs over, the one named last changes fastest.
Arguments:
- hidden: bfloat16 [1024, 8192], P('pool', 'tp'), may hold values from -6 to 6
- queries: bfloat16 [1024, 8192], P('pool', 'tp'), may hold values from -6 to 6
- key_value_weight: bfloat16 [8192, 8, 256], P('tp'), may hold values from -0.0625 to 0.0625
- adapter_down_maps: bfloat16 [256, 8192, 128], P('pool', 'tp'), may hold values from -0.0625 to 0.0625
- adapter_up_maps: bfloat16 [256, 2, 64, 8, 128], P('pool', None, None, 'tp'), may hold values from -0.75 to 0.75
- key_value_pages: bfloat16 [8704, 16, 8, 256], P('pool', None, 'tp'), may hold values from -6 to 6
- row_adapter_index: int32 [1024], P('pool'), may hold values from 0 to 255, as said below
- adapter_page_position: int32 [256], replicated, may hold values from 0 to 255, as said below
- row_page_table: int32 [1024, 16], P('pool'), may hold values from 0 to 271, as said below
- cached_length: int32 [1024], P('pool'), may hold values from 1 to 256, as said below
Outputs:
- new_kv: bfloat16 [1024, 8, 256], P('pool', 'tp')
- attended: bfloat16 [1024, 8192], P('pool', 'tp')
The draws below stay inside these ranges and needn't reach their ends.
Inputs may be any that keep to these rules, and one draw needn't show every extreme that they name: `row_adapter_index`: of the rows of one pool device, at most 2 use adapters whose pages stand on any one pool device; on one pool device stand the adapters of exactly 2 rows of every device. `adapter_page_position`: a permutation; adapter a's pages stand on pool device adapter_page_position[a] // 8, at local index adapter_page_position[a] % 8. `row_page_table`: entries are pages of the row's own pool device; row r's cached position p lies in entry p // 16; the pages used by the rows of one device are distinct and number exactly 272; entries past a row's length are arbitrary pages. `cached_length`: every pool device has a row of exactly 256 positions.
All inputs are finite; a program needn't handle non-finite values.
Results may differ from the reference program's by a relative error of at most 0.0055.
Values may be sent and summed in bfloat16 or wider, within the bound.
A program may use at most 128 MiB of HBM per device.

```python
import math
import jax
import jax.numpy as jnp
from jax import lax

MODEL_WIDTH = 8192
HQ = 64
KEY_VALUE_HEADS = 8
HEAD_SIZE = 128
ADAPTER_RANK = 64
PAGE = 16
MAXP = 16
ROWS_DEV = 32
ADP_DEV = 8
CAP = 2
NPAGES_DEV = 272
ROWS = 1024
ADAPTER_COUNT = 256
PAGES = 8704
N_POOL = 32


def page_plan(key):
    key = jax.random.fold_in(key, 501)
    first_key, order_key, tail_key, table_key, filler_key = jax.random.split(key, 5)
    pool_width = ROWS // ROWS_DEV
    half_rows = ROWS_DEV // 2
    first_half = jax.random.randint(first_key, (pool_width, half_rows), 1, MAXP + 1)
    first_half = first_half.at[:, 0].set(MAXP)
    counts = jnp.concatenate([first_half, MAXP + 1 - first_half], axis=1)
    tail_len = jax.random.randint(tail_key, (pool_width, ROWS_DEV), 1, PAGE + 1)
    tail_len = tail_len.at[:, 0].set(PAGE)

    def shuffle_rows(subkey):
        return jax.random.permutation(subkey, ROWS_DEV)
    orders = jax.vmap(shuffle_rows)(jax.random.split(order_key, pool_width))
    counts = jnp.take_along_axis(counts, orders, axis=1)
    tail_len = jnp.take_along_axis(tail_len, orders, axis=1)
    return (counts, tail_len, table_key, filler_key)


def adapter_layout(key):
    key = jax.random.fold_in(key, 601)
    return jax.random.permutation(key, ADAPTER_COUNT)


def draw_queries(key, part):
    key = jax.random.fold_in(key, 11)
    return jnp.clip(jax.random.normal(key, (ROWS, HQ * HEAD_SIZE), jnp.float32), -6.0, 6.0).astype(jnp.bfloat16)


def draw_key_value_pages(key, part):
    key = jax.random.fold_in(key, 13)
    return jnp.clip(jax.random.normal(key, (PAGES, PAGE, KEY_VALUE_HEADS, 2 * HEAD_SIZE), jnp.float32), -6.0, 6.0).astype(jnp.bfloat16)


def draw_cached_length(key, part):
    counts, tail_len, table_key, filler_key = page_plan(key)
    lengths = (counts - 1) * PAGE + tail_len
    return lengths.reshape(ROWS).astype(jnp.int32)


def draw_row_page_table(key, part):
    counts, tail_len, table_key, filler_key = page_plan(key)
    pool_width = ROWS // ROWS_DEV

    def shuffle_pages(subkey):
        return jax.random.permutation(subkey, NPAGES_DEV)
    perms = jax.vmap(shuffle_pages)(jax.random.split(table_key, pool_width))
    starts = jnp.cumsum(counts, axis=1) - counts
    column = jnp.arange(MAXP)
    entry_index = starts[:, :, None] + column[None, None, :]
    is_used = column[None, None, :] < counts[:, :, None]
    picked = jnp.take_along_axis(perms, jnp.minimum(entry_index, NPAGES_DEV - 1).reshape(pool_width, ROWS_DEV * MAXP), axis=1)
    picked = picked.reshape(pool_width, ROWS_DEV, MAXP)
    filler = jax.random.randint(filler_key, (pool_width, ROWS_DEV, MAXP), 0, NPAGES_DEV)
    return jnp.where(is_used, picked, filler).reshape(ROWS, MAXP).astype(jnp.int32)


def draw_adapter_page_position(key, part):
    return adapter_layout(key).astype(jnp.int32)


def draw_row_adapter_index(key, part):
    layout = adapter_layout(key)
    inverse = jnp.argsort(layout)
    key = jax.random.fold_in(key, 7)
    hot_key, pick_key, local_key = jax.random.split(key, 3)
    pool_width = ROWS // ROWS_DEV
    hot_owner = jax.random.randint(hot_key, (), 0, pool_width)
    others = jnp.arange((pool_width - 1) * CAP, dtype=jnp.int32) // CAP
    others = others + (others >= hot_owner).astype(jnp.int32)

    def device_owners(subkey):
        first_key, second_key = jax.random.split(subkey)
        chosen = jax.random.permutation(first_key, others)[:ROWS_DEV - CAP]
        joined = jnp.concatenate([chosen, jnp.full((CAP,), hot_owner, dtype=jnp.int32)])
        return jax.random.permutation(second_key, joined)
    owners = jax.vmap(device_owners)(jax.random.split(pick_key, pool_width))
    local_page = jax.random.randint(local_key, (pool_width, ROWS_DEV), 0, ADP_DEV)
    position = owners * ADP_DEV + local_page
    return inverse[position].reshape(ROWS).astype(jnp.int32)


def shard_levels(key, shape, shards, low, high):
    loudness, own = 1.0, jax.random.fold_in(key, 6)
    for axis_at, parts in shards:
        steps = jnp.exp(jax.random.uniform(jax.random.fold_in(own, axis_at), (parts,), jnp.float32, low / len(shards), high / len(shards)))
        loudness = loudness * jnp.repeat(steps, shape[axis_at] // parts).reshape([-1 if axis == axis_at else 1 for axis in range(len(shape))])
    return loudness


def scatter_about(stream_key, extent, scale, bound, pieces=(), held_as=jnp.bfloat16):
    array = jax.random.normal(stream_key, extent, jnp.float32) * scale
    if len(pieces) > 0:
        array = shard_levels(stream_key, extent, pieces, -0.22, 0.18) * array
    return jnp.clip(array, min=-bound, max=bound).astype(held_as)


def setup_inputs(seed: int = 0) -> dict:
    splits = jax.random.split(jax.random.key(seed), 11)
    return {
        "hidden": scatter_about(splits[0], (ROWS, MODEL_WIDTH), 1.0, 6.0, ((0, 32), (1, 8))),
        "queries": draw_queries(jax.random.fold_in(splits[10], 71), 0),
        "key_value_weight": scatter_about(splits[2], (MODEL_WIDTH, KEY_VALUE_HEADS, 2 * HEAD_SIZE), MODEL_WIDTH ** -0.5, 0.0625, ((0, 8),)),
        "adapter_down_maps": scatter_about(splits[3], (ADAPTER_COUNT, MODEL_WIDTH, 2 * ADAPTER_RANK), MODEL_WIDTH ** -0.5, 0.0625, ((0, 32), (1, 8))),
        "adapter_up_maps": scatter_about(splits[4], (ADAPTER_COUNT, 2, ADAPTER_RANK, KEY_VALUE_HEADS, HEAD_SIZE), ADAPTER_RANK ** -0.5, 0.75, ((0, 32), (3, 8))),
        "key_value_pages": draw_key_value_pages(jax.random.fold_in(splits[10], 71), 0),
        "row_adapter_index": draw_row_adapter_index(jax.random.fold_in(splits[10], 71), 0),
        "adapter_page_position": draw_adapter_page_position(jax.random.fold_in(splits[10], 71), 0),
        "row_page_table": draw_row_page_table(jax.random.fold_in(splits[10], 71), 0),
        "cached_length": draw_cached_length(jax.random.fold_in(splits[10], 71), 0),
    }


adapter_scale = 0.5

def reference(hidden, queries, key_value_weight, adapter_down_maps, adapter_up_maps, key_value_pages, row_adapter_index, adapter_page_position, row_page_table, cached_length):
    base_kv = jnp.dot(hidden, key_value_weight.reshape(MODEL_WIDTH, KEY_VALUE_HEADS * 2 * HEAD_SIZE), preferred_element_type=jnp.float32).reshape(ROWS, KEY_VALUE_HEADS, 2 * HEAD_SIZE)
    position = adapter_page_position[row_adapter_index].astype(jnp.int32)

    def one_row(items):
        features, page_position_index = items
        down_map_page = lax.dynamic_index_in_dim(adapter_down_maps, page_position_index, 0, keepdims=False)
        shrink = jnp.dot(features, down_map_page, preferred_element_type=jnp.float32).astype(jnp.bfloat16)
        up_map_page = lax.dynamic_index_in_dim(adapter_up_maps, page_position_index, 0, keepdims=False)
        key_portion = jnp.dot(shrink[:ADAPTER_RANK], up_map_page[0].reshape(ADAPTER_RANK, KEY_VALUE_HEADS * HEAD_SIZE), preferred_element_type=jnp.float32).reshape(KEY_VALUE_HEADS, HEAD_SIZE)
        value_portion = jnp.dot(shrink[ADAPTER_RANK:], up_map_page[1].reshape(ADAPTER_RANK, KEY_VALUE_HEADS * HEAD_SIZE), preferred_element_type=jnp.float32).reshape(KEY_VALUE_HEADS, HEAD_SIZE)
        return (jnp.concatenate([key_portion, value_portion], axis=1) * adapter_scale).astype(jnp.bfloat16)
    delta_kv = lax.map(one_row, (hidden, position))
    new_kv = (base_kv + delta_kv.astype(jnp.float32)).astype(jnp.bfloat16)
    cache_span = MAXP * PAGE
    blocks = (queries.reshape(N_POOL, ROWS_DEV, KEY_VALUE_HEADS, HQ // KEY_VALUE_HEADS, HEAD_SIZE), new_kv.reshape(N_POOL, ROWS_DEV, KEY_VALUE_HEADS, 2 * HEAD_SIZE), row_page_table.reshape(N_POOL, ROWS_DEV, MAXP), cached_length.reshape(N_POOL, ROWS_DEV), key_value_pages.reshape(N_POOL, NPAGES_DEV, PAGE, KEY_VALUE_HEADS, 2 * HEAD_SIZE))

    def one_block(items):
        query_heads, fresh, table, row_length, pages = items
        gathered = pages[table].reshape(ROWS_DEV, cache_span, KEY_VALUE_HEADS, 2 * HEAD_SIZE)
        every_kv = jnp.concatenate([gathered, fresh[:, None]], axis=1)
        scores = jnp.einsum('rkgd,rpkd->rkgp', query_heads.astype(jnp.float32), every_kv[..., :HEAD_SIZE].astype(jnp.float32)) * (1.0 / math.sqrt(HEAD_SIZE))
        position_id = jnp.arange(cache_span + 1, dtype=jnp.int32)
        is_valid = (position_id[None, :] < row_length[:, None]) | (position_id[None, :] == cache_span)
        is_valid = is_valid[:, None, None, :]
        row_max = lax.optimization_barrier(jnp.max(jnp.where(is_valid, scores, -jnp.inf), axis=3, keepdims=True))
        weights = jnp.where(is_valid, jnp.exp(scores - row_max), 0.0)
        weight_sum = lax.optimization_barrier(jnp.sum(weights, axis=3))
        rounded = lax.optimization_barrier(weights.astype(jnp.bfloat16)).astype(jnp.float32)
        blended = jnp.einsum('rkgp,rpkd->rkgd', rounded, every_kv[..., HEAD_SIZE:].astype(jnp.float32))
        return (blended / weight_sum[..., None]).astype(jnp.bfloat16).reshape(ROWS_DEV, HQ * HEAD_SIZE)
    attended = lax.map(one_block, blocks).reshape(ROWS, HQ * HEAD_SIZE)
    return (new_kv, attended)
```

```python
import functools
import math

import jax
import jax.numpy as jnp
from jax import lax
from jax.experimental import pallas as pl
from jax.experimental.pallas import tpu as pltpu
from jax.sharding import PartitionSpec as P

adapter_scale = 0.5
MESH = pl.DeviceIdType.MESH
LANES = 128
CAP = 2
NEG = -1e30
F32 = jnp.float32
BF16 = jnp.bfloat16


def iota(shape, dim):
    return lax.broadcasted_iota(jnp.int32, shape, dim)


def ring(extent, step):
    return min(step, extent - step)


def pool_offsets(dims):
    ny, nx, nc = dims
    steps = [(a, b, c) for a in range(ny) for b in range(nx) for c in range(nc)][1:]
    return sorted(steps, key=lambda s: -(ring(ny, s[0]) + ring(nx, s[1])) * 2 - s[2])


def pool_partner(me, dims, step):
    ny, nx, nc = dims
    y = lax.rem(me // (nx * nc) + step[0], ny)
    x = lax.rem(lax.rem(me // nc, nx) + step[1], nx)
    c = lax.rem(lax.rem(me, nc) + step[2], nc)
    return (y * nx + x) * nc + c


def kernel(
    dims,
    heads,
    hid_hbm,
    q_hbm,
    w_hbm,
    down_hbm,
    up_hbm,
    pages_hbm,
    rai_hbm,
    app_hbm,
    table_hbm,
    length_hbm,
    new_kv_ref,
    attended_ref,
    hid,
    q,
    w,
    down,
    up,
    pages,
    rai,
    app,
    table,
    length,
    send_rows,
    recv_rows,
    row_f32,
    meta_f32,
    send_base,
    recv_base,
    send_rank,
    recv_rank,
    send_delta,
    recv_delta,
    bias,
    scores,
    load_sem,
    row_send_sem,
    row_recv_sem,
    base_send_sem,
    base_recv_sem,
    rank_send_sem,
    rank_recv_sem,
    delta_send_sem,
    delta_recv_sem,
):
    me = lax.axis_index("pool")
    tp = lax.axis_index("tp")
    n_pool = dims[0] * dims[1] * dims[2]
    n_tp = heads
    rows, feats = hid.shape
    chunks = feats // LANES
    adapters = down.shape[0] // feats
    head = LANES
    group = q.shape[1] // head
    slots = CAP * n_pool
    span = CAP * chunks
    offsets = pool_offsets(dims)
    partners = [pool_partner(me, dims, s) for s in offsets]
    tp_partners = [lax.rem(tp + s, n_tp) for s in range(1, n_tp)]

    loads = [
        pltpu.make_async_copy(src, dst, load_sem.at[i])
        for i, (src, dst) in enumerate(
            (
                (rai_hbm, rai),
                (app_hbm, app),
                (hid_hbm, hid),
                (w_hbm, w),
                (table_hbm, table),
                (length_hbm, length),
                (q_hbm, q),
                (down_hbm, down),
                (pages_hbm, pages),
                (up_hbm, up),
            )
        )
    ]
    (l_rai, l_app, l_hid, l_w, l_table, l_length, l_q, l_down, l_pages, l_up) = loads
    for load in loads:
        load.start()

    barrier = pltpu.get_barrier_semaphore()
    for p in partners:
        pl.semaphore_signal(barrier, inc=1, device_id=(p, tp), device_id_type=MESH)
    for t in tp_partners:
        pl.semaphore_signal(barrier, inc=1, device_id=(me, t), device_id_type=MESH)

    l_rai.wait()
    l_app.wait()
    eye = iota((rows, rows), 0) == iota((rows, rows), 1)
    rai_row = rai[...].astype(F32)
    rai_col = jnp.sum(jnp.where(eye, rai_row, 0.0), axis=1, keepdims=True)
    n_adapters = app.shape[1]
    hit = rai_col == iota((rows, n_adapters), 1).astype(F32)
    position = jnp.sum(jnp.where(hit, app[...].astype(F32), 0.0), axis=1, keepdims=True)
    owner = jnp.floor(position * (1.0 / adapters))
    local = position - owner * adapters
    owner_row = jnp.sum(jnp.where(eye, owner, 0.0), axis=0, keepdims=True)
    earlier = iota((rows, rows), 1) < iota((rows, rows), 0)
    rank = jnp.sum(jnp.where((owner == owner_row) & earlier, 1.0, 0.0), axis=1, keepdims=True)
    target = owner * CAP + rank

    lanes = chunks * rows
    lane_eye = iota((rows, lanes), 0) == lax.rem(iota((rows, lanes), 1), rows)
    target_lane = jnp.sum(jnp.where(lane_eye, target, 0.0), axis=0, keepdims=True)
    line = iota((slots * chunks, lanes), 0)
    place = ((line // chunks).astype(F32) == target_lane) & (
        lax.rem(line, chunks) == iota((slots * chunks, lanes), 1) // rows
    )
    place = jnp.where(place, 1.0, 0.0).astype(BF16)
    l_hid.wait()
    stacked = jnp.concatenate([hid[:, c * LANES : (c + 1) * LANES] for c in range(chunks)], axis=0)
    local_lines = jnp.broadcast_to(local, (rows, LANES)).astype(BF16)
    local_stack = jnp.concatenate([local_lines] * chunks, axis=0)
    packets = jnp.dot(
        place, jnp.concatenate([stacked, local_stack], axis=1), preferred_element_type=F32
    ).astype(BF16)
    send_rows[:, 0:span, :] = packets[:, :LANES].reshape(n_pool, span, LANES)
    send_rows[:, span : 2 * span, :] = packets[:, LANES:].reshape(n_pool, span, LANES)

    pl.semaphore_wait(barrier, len(partners) + len(tp_partners))

    row_copies = []
    for k, p in enumerate(partners):
        copy = pltpu.make_async_remote_copy(
            src_ref=send_rows.at[p],
            dst_ref=recv_rows.at[me],
            send_sem=row_send_sem.at[k],
            recv_sem=row_recv_sem.at[k],
            device_id=(p, tp),
            device_id_type=MESH,
        )
        copy.start()
        row_copies.append(copy)
    recv_rows[me] = send_rows[me]

    wide = LANES * heads
    spread = iota((LANES, wide), 0) == iota((LANES, wide), 1) // heads
    spread = jnp.where(spread, 1.0, 0.0).astype(BF16)
    repeated = jnp.dot(stacked, spread, preferred_element_type=F32).astype(BF16)
    head_of_lane = lax.rem(iota((rows, wide), 1), heads)
    l_w.wait()
    base = jnp.zeros((heads * rows, 2 * head), F32)
    for c in range(chunks):
        piece = repeated[c * rows : (c + 1) * rows, :]
        masked = jnp.concatenate(
            [jnp.where(head_of_lane == g, piece, jnp.zeros_like(piece)) for g in range(heads)], axis=0
        )
        base += jnp.dot(masked, w[c * wide : (c + 1) * wide, :], preferred_element_type=F32)
    send_base[...] = base.astype(BF16).reshape(heads, rows, 2 * head)
    base_copies = []
    for k, t in enumerate(tp_partners):
        copy = pltpu.make_async_remote_copy(
            src_ref=send_base.at[t],
            dst_ref=recv_base.at[tp],
            send_sem=base_send_sem.at[k],
            recv_sem=base_recv_sem.at[k],
            device_id=(me, t),
            device_id_type=MESH,
        )
        copy.start()
        base_copies.append(copy)
    recv_base[tp] = send_base[tp]

    l_down.wait()
    for copy in row_copies:
        copy.wait_recv()
    row_f32[...] = recv_rows[:, 0:span, :].astype(F32).reshape(n_pool * span, LANES)
    meta_f32[...] = recv_rows[:, span : 2 * span, :].astype(F32).reshape(n_pool * span, LANES)
    taken = jnp.concatenate(
        [
            jnp.concatenate(
                [row_f32[pl.ds(s * chunks + c, n_pool, stride=span), :] for c in range(chunks)], axis=1
            )
            for s in range(CAP)
        ],
        axis=0,
    ).astype(BF16)
    adapter_of = jnp.concatenate(
        [meta_f32[pl.ds(s * chunks, n_pool, stride=span), :] for s in range(CAP)], axis=0
    )
    partial = jnp.zeros((slots, LANES), F32)
    for a in range(adapters):
        product = jnp.dot(taken, down[a * feats : (a + 1) * feats, :], preferred_element_type=F32)
        partial = jnp.where(adapter_of == float(a), product, partial)
    send_rank[...] = partial.astype(BF16)
    rank_copies = []
    for k, t in enumerate(tp_partners):
        copy = pltpu.make_async_remote_copy(
            src_ref=send_rank,
            dst_ref=recv_rank.at[tp],
            send_sem=rank_send_sem.at[k],
            recv_sem=rank_recv_sem.at[k],
            device_id=(me, t),
            device_id_type=MESH,
        )
        copy.start()
        rank_copies.append(copy)
    recv_rank[tp] = send_rank[...]

    l_table.wait()
    l_length.wait()
    entries, _ = table.shape
    positions = pages.shape[0]
    page = 16
    eye_bf16 = jnp.where(eye, 1.0, 0.0).astype(BF16)
    entry = table[...]
    high, low = entry // 16, lax.rem(entry, 16)
    turn = (((1,), (1,)), ((), ()))
    table_rows = (
        lax.dot_general(eye_bf16, high.astype(F32).astype(BF16), turn, preferred_element_type=F32) * 16.0
        + lax.dot_general(eye_bf16, low.astype(F32).astype(BF16), turn, preferred_element_type=F32)
    )
    length_col = jnp.sum(jnp.where(eye, length[...].astype(F32), 0.0), axis=1, keepdims=True)
    page_blocks = pl.cdiv(positions // page, LANES)
    page_id = iota((rows, page_blocks * LANES), 1).astype(F32)
    held = jnp.zeros((rows, page_blocks * LANES), F32)
    for j in range(entries):
        valid = jnp.clip(length_col - float(page * j), 0.0, float(page))
        held += jnp.where(table_rows[:, j : j + 1] == page_id, valid, 0.0)
    held = held.astype(BF16)
    widen = iota((LANES, LANES * page), 0) == iota((LANES, LANES * page), 1) // page
    widen = jnp.where(widen, 1.0, 0.0).astype(BF16)
    for b in range(page_blocks):
        first = b * LANES * page
        width = min(LANES * page, positions - first)
        count = jnp.dot(held[:, b * LANES : (b + 1) * LANES], widen[:, :width], preferred_element_type=F32)
        within = lax.rem(iota((rows, width), 1), page).astype(F32)
        bias[:, first : first + width] = jnp.where(within < count, 0.0, NEG)

    l_q.wait()
    l_pages.wait()
    query = jnp.concatenate([q[:, h * head : (h + 1) * head] for h in range(group)], axis=0)
    scale = math.log2(math.e) / math.sqrt(head)
    tile = 256
    tiles = positions // tile
    pairs = group * rows

    def score_step(j, largest):
        at = pl.ds(pl.multiple_of(j * tile, tile), tile)
        s = lax.dot_general(query, pages[at, 0:head], turn, preferred_element_type=F32) * scale
        s = (s.reshape(group, rows, tile) + bias[:, at][None]).reshape(pairs, tile)
        scores[j] = s
        return jnp.maximum(largest, jnp.maximum(s[:, :LANES], s[:, LANES:]))

    largest = lax.fori_loop(0, tiles, score_step, jnp.full((pairs, LANES), NEG, F32))
    largest = jnp.max(largest, axis=1, keepdims=True)

    def weight_step(j, carry):
        total, blended = carry
        at = pl.ds(pl.multiple_of(j * tile, tile), tile)
        weight = jnp.exp2(scores[j] - largest)
        total = total + weight[:, :LANES] + weight[:, LANES:]
        blended = blended + jnp.dot(
            weight.astype(BF16), pages[at, head : 2 * head], preferred_element_type=F32
        )
        return total, blended

    l_up.wait()
    for copy in rank_copies:
        copy.wait_recv()
    shrink = recv_rank[0].astype(F32)
    for t in range(1, n_tp):
        shrink += recv_rank[t].astype(F32)
    shrink = shrink.astype(BF16).astype(F32)
    key_lane = iota((slots, LANES), 1) < LANES // 2
    halves = [
        jnp.concatenate(
            [jnp.where((adapter_of == float(a)) & lane, shrink, 0.0) for a in range(adapters)], axis=1
        )
        for lane in (key_lane, jnp.logical_not(key_lane))
    ]
    delta = jnp.dot(jnp.concatenate(halves, axis=0).astype(BF16), up[...], preferred_element_type=F32)
    delta = (delta * adapter_scale).astype(BF16).astype(F32)
    for s in range(CAP):
        for half in range(2):
            first = half * slots + s * n_pool
            send_delta[pl.ds(s * 2 + half, n_pool, stride=8), :] = delta[first : first + n_pool, :]
    for blank in range(2 * CAP, 8):
        send_delta[pl.ds(blank, n_pool, stride=8), :] = jnp.zeros((n_pool, LANES), F32)
    delta_copies = []
    mine = pl.ds(pl.multiple_of(me * 8, 8), 8)
    for k, p in enumerate(partners):
        copy = pltpu.make_async_remote_copy(
            src_ref=send_delta.at[pl.ds(pl.multiple_of(p * 8, 8), 8)],
            dst_ref=recv_delta.at[mine],
            send_sem=delta_send_sem.at[k],
            recv_sem=delta_recv_sem.at[k],
            device_id=(p, tp),
            device_id_type=MESH,
        )
        copy.start()
        delta_copies.append(copy)
    recv_delta[mine, :] = send_delta[mine, :]

    zero = jnp.zeros((pairs, LANES), F32)
    total, blended = lax.fori_loop(0, tiles, weight_step, (zero, zero))
    total = jnp.sum(total, axis=1, keepdims=True)

    for copy in base_copies:
        copy.wait_recv()
    base = recv_base[0].astype(F32)
    for t in range(1, n_tp):
        base += recv_base[t].astype(F32)
    column = iota((rows, 8 * n_pool), 1)
    slot_of = (column // 8) * CAP + lax.rem(column, 8) // 2
    live = lax.rem(column, 8) < 2 * CAP
    picks = [
        (slot_of.astype(F32) == target) & live & (lax.rem(column, 2) == half) for half in range(2)
    ]
    pick = jnp.concatenate([jnp.where(m, 1.0, 0.0) for m in picks], axis=0).astype(BF16)
    for copy in delta_copies:
        copy.wait_recv()
    rows_delta = jnp.dot(pick, recv_delta[...].astype(BF16), preferred_element_type=F32)
    new_key = (base[:, :head] + rows_delta[:rows]).astype(BF16)
    new_value = (base[:, head:] + rows_delta[rows:]).astype(BF16)
    new_kv_ref[:, :head] = new_key
    new_kv_ref[:, head:] = new_value
    new_key, new_value = new_key.astype(F32)[None], new_value.astype(F32)[None]
    own = jnp.sum(
        (query.astype(F32).reshape(group, rows, head) * new_key).reshape(pairs, head), axis=1, keepdims=True
    ) * scale
    top = jnp.maximum(largest, own)
    fade = jnp.exp2(largest - top)
    own = jnp.exp2(own - top)
    total = total * fade + own
    rounded = own.astype(BF16).astype(F32)
    spread_own = jnp.broadcast_to(rounded, (pairs, head)).reshape(group, rows, head) * new_value
    result = (blended * fade + spread_own.reshape(pairs, head)) / total
    for h in range(group):
        attended_ref[:, h * head : (h + 1) * head] = result[h * rows : (h + 1) * rows].astype(BF16)

    for copy in row_copies + base_copies + rank_copies + delta_copies:
        copy.wait_send()


def body(
    dims,
    hidden,
    queries,
    key_value_weight,
    adapter_down_maps,
    adapter_up_maps,
    key_value_pages,
    row_adapter_index,
    adapter_page_position,
    row_page_table,
    cached_length,
):
    rows, feats = hidden.shape
    heads = key_value_weight.shape[1]
    width = key_value_weight.shape[2]
    adapters, _, double_rank = adapter_down_maps.shape
    n_pages, page = key_value_pages.shape[:2]
    n_pool = dims[0] * dims[1] * dims[2]
    positions = n_pages * page
    slots = CAP * n_pool
    span = CAP * feats // LANES
    pairs = rows * queries.shape[1] // LANES
    operands = (
        hidden,
        queries,
        key_value_weight.reshape(feats * heads, width),
        adapter_down_maps.reshape(adapters * feats, double_rank),
        adapter_up_maps.reshape(adapters * double_rank, width // 2),
        key_value_pages.reshape(positions, width),
        row_adapter_index.reshape(1, rows),
        adapter_page_position.reshape(1, -1),
        row_page_table.T,
        cached_length.reshape(1, rows),
    )
    vmem = [pltpu.VMEM(x.shape, x.dtype) for x in operands]
    scratch = vmem + [
        pltpu.VMEM((n_pool, 2 * span, LANES), BF16),
        pltpu.VMEM((n_pool, 2 * span, LANES), BF16),
        pltpu.VMEM((n_pool * span, LANES), F32),
        pltpu.VMEM((n_pool * span, LANES), F32),
        pltpu.VMEM((heads, rows, width), BF16),
        pltpu.VMEM((heads, rows, width), BF16),
        pltpu.VMEM((slots, LANES), BF16),
        pltpu.VMEM((heads, slots, LANES), BF16),
        pltpu.VMEM((n_pool * 8, LANES), F32),
        pltpu.VMEM((n_pool * 8, LANES), F32),
        pltpu.VMEM((rows, positions), F32),
        pltpu.VMEM((positions // 256, pairs, 256), F32),
        pltpu.SemaphoreType.DMA((len(operands),)),
        pltpu.SemaphoreType.DMA((n_pool - 1,)),
        pltpu.SemaphoreType.DMA((n_pool - 1,)),
        pltpu.SemaphoreType.DMA((heads - 1,)),
        pltpu.SemaphoreType.DMA((heads - 1,)),
        pltpu.SemaphoreType.DMA((heads - 1,)),
        pltpu.SemaphoreType.DMA((heads - 1,)),
        pltpu.SemaphoreType.DMA((n_pool - 1,)),
        pltpu.SemaphoreType.DMA((n_pool - 1,)),
    ]
    new_kv, attended = pl.pallas_call(
        functools.partial(kernel, dims, heads),
        out_shape=(
            jax.ShapeDtypeStruct((rows, width), BF16),
            jax.ShapeDtypeStruct(queries.shape, BF16),
        ),
        in_specs=[pl.BlockSpec(memory_space=pl.ANY)] * len(operands),
        out_specs=(pl.BlockSpec(memory_space=pltpu.VMEM),) * 2,
        scratch_shapes=scratch,
        compiler_params=pltpu.CompilerParams(
            collective_id=0, has_side_effects=True, vmem_limit_bytes=60 * 1024 * 1024
        ),
        name="decode_step",
    )(*operands)
    return new_kv.reshape(rows, 1, width), attended


def solution(mesh):
    placed = (
        P("pool", "tp"),
        P("pool", "tp"),
        P("tp", None, None),
        P("pool", "tp", None),
        P("pool", None, None, "tp", None),
        P("pool", None, "tp", None),
        P("pool"),
        P(),
        P("pool", None),
        P("pool"),
    )
    n_pool = mesh.shape["pool"]
    dims = (4, 4, 2) if n_pool == 32 else (1, n_pool // 2, 2)
    return jax.shard_map(
        functools.partial(body, dims),
        mesh=mesh,
        in_specs=placed,
        out_specs=(P("pool", "tp", None), P("pool", "tp")),
        check_vma=False,
    )
```

```python
import functools
import math

import jax
import jax.numpy as jnp
from jax import lax
from jax.experimental import pallas as pl
from jax.experimental.pallas import tpu as pltpu
from jax.sharding import PartitionSpec as P

adapter_scale = 0.5
MESH = pl.DeviceIdType.MESH
LANES = 128
CAP = 2
NEG = -1e30
F32 = jnp.float32
BF16 = jnp.bfloat16


def iota(shape, dim):
    return lax.broadcasted_iota(jnp.int32, shape, dim)


def ring(extent, step):
    return min(step, extent - step)


def pool_offsets(dims):
    ny, nx, nc = dims
    steps = [(a, b, c) for a in range(ny) for b in range(nx) for c in range(nc)][1:]
    return sorted(steps, key=lambda s: -(ring(ny, s[0]) + ring(nx, s[1])) * 2 - s[2])


def pool_partner(me, dims, step):
    ny, nx, nc = dims
    y = lax.rem(me // (nx * nc) + step[0], ny)
    x = lax.rem(lax.rem(me // nc, nx) + step[1], nx)
    c = lax.rem(lax.rem(me, nc) + step[2], nc)
    return (y * nx + x) * nc + c


def wait_bytes(ref, sem):
    pltpu.make_async_copy(ref, ref, sem).wait()


def kernel(
    dims,
    heads,
    hid_hbm,
    q_hbm,
    w_hbm,
    down_hbm,
    up_hbm,
    pages_hbm,
    rai_hbm,
    app_hbm,
    table_hbm,
    length_hbm,
    new_kv_ref,
    attended_ref,
    hid,
    q,
    w,
    down,
    up,
    pages,
    rai,
    app,
    table,
    length,
    send_rows,
    recv_rows,
    send_meta,
    recv_meta,
    row_f32,
    send_base,
    recv_base,
    send_rank,
    recv_rank,
    up_mask,
    delta_lines,
    send_delta,
    recv_delta,
    bias,
    scores,
    load_sem,
    row_sems,
    meta_sems,
    base_sems,
    rank_sems,
    delta_sems,
):
    me = lax.axis_index("pool")
    tp = lax.axis_index("tp")
    n_pool = dims[0] * dims[1] * dims[2]
    n_tp = heads
    rows, feats = hid.shape
    chunks = feats // LANES
    adapters = down.shape[0] // feats
    head = LANES
    group = q.shape[1] // head
    slots = CAP * n_pool
    span = CAP * chunks
    offsets = pool_offsets(dims)
    partners = [pool_partner(me, dims, s) for s in offsets]
    tp_steps = sorted(range(1, n_tp), key=lambda s: -ring(n_tp, s))
    tp_partners = [lax.rem(tp + s, n_tp) for s in tp_steps]

    loads = [
        pltpu.make_async_copy(src, dst, load_sem.at[i])
        for i, (src, dst) in enumerate(
            (
                (rai_hbm, rai),
                (app_hbm, app),
                (hid_hbm, hid),
                (w_hbm, w),
                (table_hbm, table),
                (length_hbm, length),
                (q_hbm, q),
                (down_hbm, down),
                (pages_hbm, pages),
                (up_hbm, up),
            )
        )
    ]
    (l_rai, l_app, l_hid, l_w, l_table, l_length, l_q, l_down, l_pages, l_up) = loads
    barrier = pltpu.get_barrier_semaphore()
    for t in tp_partners:
        pl.semaphore_signal(barrier, inc=1, device_id=(me, t), device_id_type=MESH)
    for p in partners:
        pl.semaphore_signal(barrier, inc=1, device_id=(p, tp), device_id_type=MESH)
    for load in loads:
        load.start()

    l_rai.wait()
    l_app.wait()
    eye = iota((rows, rows), 0) == iota((rows, rows), 1)
    rai_row = rai[...].astype(F32)
    rai_col = jnp.sum(jnp.where(eye, rai_row, 0.0), axis=1, keepdims=True)
    n_adapters = app.shape[1]
    hit = rai_col == iota((rows, n_adapters), 1).astype(F32)
    position = jnp.sum(jnp.where(hit, app[...].astype(F32), 0.0), axis=1, keepdims=True)
    owner = jnp.floor(position * (1.0 / adapters))
    local = position - owner * adapters
    owner_row = jnp.sum(jnp.where(eye, owner, 0.0), axis=0, keepdims=True)
    earlier = iota((rows, rows), 1) < iota((rows, rows), 0)
    rank = jnp.sum(jnp.where((owner == owner_row) & earlier, 1.0, 0.0), axis=1, keepdims=True)
    target = owner * CAP + rank

    lanes = chunks * rows
    lane_eye = iota((rows, lanes), 0) == lax.rem(iota((rows, lanes), 1), rows)
    target_lane = jnp.sum(jnp.where(lane_eye, target, 0.0), axis=0, keepdims=True)
    line = iota((slots * chunks, lanes), 0)
    place = ((line // chunks).astype(F32) == target_lane) & (
        lax.rem(line, chunks) == iota((slots * chunks, lanes), 1) // rows
    )
    place = jnp.where(place, 1.0, 0.0).astype(BF16)
    l_hid.wait()
    stacked = jnp.concatenate([hid[:, c * LANES : (c + 1) * LANES] for c in range(chunks)], axis=0)
    packets = jnp.dot(place, stacked, preferred_element_type=F32).astype(BF16)
    send_rows[...] = packets.reshape(n_pool, span, LANES)
    first_half = iota((rows, LANES), 1) < LANES // 2
    held_by = iota((n_pool, CAP * rows), 0) * CAP + iota((n_pool, CAP * rows), 1) // rows
    held_by = jnp.where(held_by.astype(F32) == target_lane[:, : CAP * rows], 1.0, 0.0).astype(BF16)
    lines = jnp.concatenate(
        [jnp.where(first_half, local, 0.0), jnp.where(first_half, 0.0, local)], axis=0
    ).astype(BF16)
    send_meta[...] = jnp.dot(held_by, lines, preferred_element_type=F32).reshape(n_pool, 1, LANES)

    pl.semaphore_wait(barrier, len(partners) + len(tp_partners))

    for p in partners:
        pltpu.make_async_remote_copy(
            src_ref=send_rows.at[p],
            dst_ref=recv_rows.at[me],
            send_sem=row_sems.at[0],
            recv_sem=row_sems.at[1],
            device_id=(p, tp),
            device_id_type=MESH,
        ).start()
        pltpu.make_async_remote_copy(
            src_ref=send_meta.at[p],
            dst_ref=recv_meta.at[me],
            send_sem=meta_sems.at[0],
            recv_sem=meta_sems.at[1],
            device_id=(p, tp),
            device_id_type=MESH,
        ).start()
    recv_rows[me] = send_rows[me]
    recv_meta[me] = send_meta[me]

    wide = LANES * heads
    spread = iota((LANES, wide), 0) == iota((LANES, wide), 1) // heads
    spread = jnp.where(spread, 1.0, 0.0).astype(BF16)
    repeated = jnp.dot(stacked, spread, preferred_element_type=F32).astype(BF16)
    head_of_lane = lax.rem(iota((rows, wide), 1), heads)
    l_w.wait()
    base = jnp.zeros((heads * rows, 2 * head), F32)
    for c in range(chunks):
        piece = repeated[c * rows : (c + 1) * rows, :]
        masked = jnp.concatenate(
            [jnp.where(head_of_lane == g, piece, jnp.zeros_like(piece)) for g in range(heads)], axis=0
        )
        base += jnp.dot(masked, w[c * wide : (c + 1) * wide, :], preferred_element_type=F32)
    send_base[...] = base.astype(BF16).reshape(heads, rows, 2 * head)
    for t in tp_partners:
        pltpu.make_async_remote_copy(
            src_ref=send_base.at[t],
            dst_ref=recv_base.at[tp],
            send_sem=base_sems.at[0],
            recv_sem=base_sems.at[1],
            device_id=(me, t),
            device_id_type=MESH,
        ).start()
    recv_base[tp] = send_base[tp]

    l_down.wait()
    others = pl.ds(0, n_pool - 1)
    wait_bytes(recv_rows.at[others], row_sems.at[1])
    wait_bytes(recv_meta.at[others], meta_sems.at[1])
    row_f32[...] = recv_rows[...].astype(F32).reshape(n_pool * span, LANES)
    taken = jnp.concatenate(
        [
            jnp.concatenate(
                [row_f32[pl.ds(s * chunks + c, n_pool, stride=span), :] for c in range(chunks)], axis=1
            )
            for s in range(CAP)
        ],
        axis=0,
    ).astype(BF16)
    meta = recv_meta[...].reshape(n_pool, LANES)
    turned = pltpu.roll(meta, LANES // 2, 1)
    first_half = iota((n_pool, LANES), 1) < LANES // 2
    adapter_of = jnp.concatenate(
        [jnp.where(first_half, meta, turned), jnp.where(first_half, turned, meta)], axis=0
    )
    partial = jnp.zeros((slots, LANES), F32)
    for a in range(0, adapters, 2):
        both = jnp.concatenate(
            [down[a * feats : (a + 1) * feats, :], down[(a + 1) * feats : (a + 2) * feats, :]], axis=1
        )
        product = jnp.dot(taken, both, preferred_element_type=F32)
        partial = jnp.where(adapter_of == float(a), product[:, :LANES], partial)
        partial = jnp.where(adapter_of == float(a + 1), product[:, LANES:], partial)
    send_rank[...] = partial.astype(BF16)
    for t in tp_partners:
        pltpu.make_async_remote_copy(
            src_ref=send_rank,
            dst_ref=recv_rank.at[tp],
            send_sem=rank_sems.at[0],
            recv_sem=rank_sems.at[1],
            device_id=(me, t),
            device_id_type=MESH,
        ).start()
    recv_rank[tp] = send_rank[...]

    l_table.wait()
    l_length.wait()
    entries, _ = table.shape
    positions = pages.shape[0]
    page = 16
    eye_bf16 = jnp.where(eye, 1.0, 0.0).astype(BF16)
    entry = table[...]
    high, low = entry // 16, lax.rem(entry, 16)
    turn = (((1,), (1,)), ((), ()))
    table_rows = (
        lax.dot_general(eye_bf16, high.astype(F32).astype(BF16), turn, preferred_element_type=F32) * 16.0
        + lax.dot_general(eye_bf16, low.astype(F32).astype(BF16), turn, preferred_element_type=F32)
    )
    length_col = jnp.sum(jnp.where(eye, length[...].astype(F32), 0.0), axis=1, keepdims=True)
    page_blocks = pl.cdiv(positions // page, LANES)
    page_id = iota((rows, page_blocks * LANES), 1).astype(F32)
    held = jnp.zeros((rows, page_blocks * LANES), F32)
    for j in range(entries):
        valid = jnp.clip(length_col - float(page * j), 0.0, float(page))
        held += jnp.where(table_rows[:, j : j + 1] == page_id, valid, 0.0)
    held = held.astype(BF16)
    widen = iota((LANES, LANES * page), 0) == iota((LANES, LANES * page), 1) // page
    widen = jnp.where(widen, 1.0, 0.0).astype(BF16)
    for b in range(page_blocks):
        first = b * LANES * page
        width = min(LANES * page, positions - first)
        count = jnp.dot(held[:, b * LANES : (b + 1) * LANES], widen[:, :width], preferred_element_type=F32)
        within = lax.rem(iota((rows, width), 1), page).astype(F32)
        bias[:, first : first + width] = jnp.where(within < count, 0.0, NEG)

    l_q.wait()
    l_pages.wait()
    query = jnp.concatenate([q[:, h * head : (h + 1) * head] for h in range(group)], axis=0)
    scale = math.log2(math.e) / math.sqrt(head)
    tile = 256
    tiles = positions // tile
    pairs = group * rows

    def score_step(j, largest):
        at = pl.ds(pl.multiple_of(j * tile, tile), tile)
        s = lax.dot_general(query, pages[at, 0:head], turn, preferred_element_type=F32) * scale
        s = (s.reshape(group, rows, tile) + bias[:, at][None]).reshape(pairs, tile)
        scores[j] = s
        return jnp.maximum(largest, jnp.maximum(s[:, :LANES], s[:, LANES:]))

    largest = lax.fori_loop(0, tiles, score_step, jnp.full((pairs, LANES), NEG, F32))
    largest = jnp.max(largest, axis=1, keepdims=True)

    def weight_step(j, carry):
        total, blended = carry
        at = pl.ds(pl.multiple_of(j * tile, tile), tile)
        weight = jnp.exp2(scores[j] - largest)
        total = total + weight[:, :LANES] + weight[:, LANES:]
        blended = blended + jnp.dot(
            weight.astype(BF16), pages[at, head : 2 * head], preferred_element_type=F32
        )
        return total, blended

    key_lane = iota((slots, LANES), 1) < LANES // 2
    for half, lane in enumerate((key_lane, jnp.logical_not(key_lane))):
        for a in range(adapters):
            on = jnp.where((adapter_of == float(a)) & lane, 1.0, 0.0).astype(BF16)
            up_mask[half * slots : (half + 1) * slots, a * LANES : (a + 1) * LANES] = on
    l_up.wait()
    wait_bytes(recv_rows.at[others], row_sems.at[0])
    wait_bytes(recv_meta.at[others], meta_sems.at[0])
    wait_bytes(recv_base.at[pl.ds(0, n_tp - 1)], base_sems.at[0])
    wait_bytes(recv_rank.at[pl.ds(0, n_tp - 1)], rank_sems.at[1])
    shrink = recv_rank[0].astype(F32)
    for t in range(1, n_tp):
        shrink += recv_rank[t].astype(F32)
    shrink = shrink.astype(BF16)
    spread_rank = jnp.concatenate([shrink] * adapters, axis=1)
    spread_rank = jnp.concatenate([spread_rank] * 2, axis=0) * up_mask[...]
    delta = jnp.dot(spread_rank, up[...], preferred_element_type=F32)
    delta = (delta * adapter_scale).astype(BF16).astype(F32)
    for s in range(CAP):
        for half in range(2):
            first = half * slots + s * n_pool
            delta_lines[pl.ds(s * 2 + half, n_pool, stride=2 * CAP), :] = delta[first : first + n_pool, :]
    send_delta[...] = delta_lines[...].reshape(n_pool, 2 * CAP, LANES)
    for p in partners:
        pltpu.make_async_remote_copy(
            src_ref=send_delta.at[p],
            dst_ref=recv_delta.at[me],
            send_sem=delta_sems.at[0],
            recv_sem=delta_sems.at[1],
            device_id=(p, tp),
            device_id_type=MESH,
        ).start()
    recv_delta[me] = send_delta[me]

    zero = jnp.zeros((pairs, LANES), F32)
    total, blended = lax.fori_loop(0, tiles, weight_step, (zero, zero))
    total = jnp.sum(total, axis=1, keepdims=True)

    wait_bytes(recv_base.at[pl.ds(0, n_tp - 1)], base_sems.at[1])
    base = recv_base[0].astype(F32)
    for t in range(1, n_tp):
        base += recv_base[t].astype(F32)
    column = iota((rows, 2 * slots), 1)
    mine = (column // 2).astype(F32) == target
    picks = [mine & (lax.rem(column, 2) == half) for half in range(2)]
    pick = jnp.concatenate([jnp.where(m, 1.0, 0.0) for m in picks], axis=0).astype(BF16)
    wait_bytes(recv_rank.at[pl.ds(0, n_tp - 1)], rank_sems.at[0])
    wait_bytes(recv_delta.at[others], delta_sems.at[1])
    arrived = recv_delta[...].reshape(2 * slots, LANES).astype(BF16)
    rows_delta = jnp.dot(pick, arrived, preferred_element_type=F32)
    new_key = (base[:, :head] + rows_delta[:rows]).astype(BF16)
    new_value = (base[:, head:] + rows_delta[rows:]).astype(BF16)
    new_kv_ref[:, :head] = new_key
    new_kv_ref[:, head:] = new_value
    new_key, new_value = new_key.astype(F32)[None], new_value.astype(F32)[None]
    own = jnp.sum(
        (query.astype(F32).reshape(group, rows, head) * new_key).reshape(pairs, head), axis=1, keepdims=True
    ) * scale
    top = jnp.maximum(largest, own)
    fade = jnp.exp2(largest - top)
    own = jnp.exp2(own - top)
    total = total * fade + own
    rounded = own.astype(BF16).astype(F32)
    spread_own = jnp.broadcast_to(rounded, (pairs, head)).reshape(group, rows, head) * new_value
    result = (blended * fade + spread_own.reshape(pairs, head)) * (1.0 / total)
    for h in range(group):
        attended_ref[:, h * head : (h + 1) * head] = result[h * rows : (h + 1) * rows].astype(BF16)

    wait_bytes(recv_delta.at[others], delta_sems.at[0])


def body(
    dims,
    hidden,
    queries,
    key_value_weight,
    adapter_down_maps,
    adapter_up_maps,
    key_value_pages,
    row_adapter_index,
    adapter_page_position,
    row_page_table,
    cached_length,
):
    rows, feats = hidden.shape
    heads = key_value_weight.shape[1]
    width = key_value_weight.shape[2]
    adapters, _, double_rank = adapter_down_maps.shape
    n_pages, page = key_value_pages.shape[:2]
    n_pool = dims[0] * dims[1] * dims[2]
    positions = n_pages * page
    slots = CAP * n_pool
    span = CAP * feats // LANES
    pairs = rows * queries.shape[1] // LANES
    operands = (
        hidden,
        queries,
        key_value_weight.reshape(feats * heads, width),
        adapter_down_maps.reshape(adapters * feats, double_rank),
        adapter_up_maps.reshape(adapters * double_rank, width // 2),
        key_value_pages.reshape(positions, width),
        row_adapter_index.reshape(1, rows),
        adapter_page_position.reshape(1, -1),
        row_page_table.T,
        cached_length.reshape(1, rows),
    )
    vmem = [pltpu.VMEM(x.shape, x.dtype) for x in operands]
    scratch = vmem + [
        pltpu.VMEM((n_pool, span, LANES), BF16),
        pltpu.VMEM((n_pool, span, LANES), BF16),
        pltpu.VMEM((n_pool, 1, LANES), F32),
        pltpu.VMEM((n_pool, 1, LANES), F32),
        pltpu.VMEM((n_pool * span, LANES), F32),
        pltpu.VMEM((heads, rows, width), BF16),
        pltpu.VMEM((heads, rows, width), BF16),
        pltpu.VMEM((slots, LANES), BF16),
        pltpu.VMEM((heads, slots, LANES), BF16),
        pltpu.VMEM((2 * slots, adapters * LANES), BF16),
        pltpu.VMEM((2 * slots, LANES), F32),
        pltpu.VMEM((n_pool, 2 * CAP, LANES), F32),
        pltpu.VMEM((n_pool, 2 * CAP, LANES), F32),
        pltpu.VMEM((rows, positions), F32),
        pltpu.VMEM((positions // 256, pairs, 256), F32),
        pltpu.SemaphoreType.DMA((len(operands),)),
        *[pltpu.SemaphoreType.DMA((2,)) for _ in range(5)],
    ]
    new_kv, attended = pl.pallas_call(
        functools.partial(kernel, dims, heads),
        out_shape=(
            pltpu.VMEM((rows, width), BF16),
            pltpu.VMEM(queries.shape, BF16),
        ),
        in_specs=[pl.BlockSpec(memory_space=pl.ANY)] * len(operands),
        out_specs=(pl.BlockSpec(memory_space=pltpu.VMEM),) * 2,
        scratch_shapes=scratch,
        compiler_params=pltpu.CompilerParams(
            collective_id=0, has_side_effects=True, vmem_limit_bytes=60 * 1024 * 1024
        ),
        name="decode_step",
    )(*operands)
    return new_kv.reshape(rows, 1, width), attended


def solution(mesh):
    placed = (
        P("pool", "tp"),
        P("pool", "tp"),
        P("tp", None, None),
        P("pool", "tp", None),
        P("pool", None, None, "tp", None),
        P("pool", None, "tp", None),
        P("pool"),
        P(),
        P("pool", None),
        P("pool"),
    )
    n_pool = mesh.shape["pool"]
    dims = (4, 4, 2) if n_pool == 32 else (1, n_pool // 2, 2)
    return jax.shard_map(
        functools.partial(body, dims),
        mesh=mesh,
        in_specs=placed,
        out_specs=(P("pool", "tp", None), P("pool", "tp")),
        check_vma=False,
    )
```

```python
import functools
import math

import jax
import jax.numpy as jnp
from jax import lax
from jax.experimental import pallas as pl
from jax.experimental.pallas import tpu as pltpu
from jax.sharding import PartitionSpec as P

adapter_scale = 0.5
MESH = pl.DeviceIdType.MESH
LANES = 128
CAP = 2
NEG = -1e30
F32 = jnp.float32
BF16 = jnp.bfloat16


def iota(shape, dim):
    return lax.broadcasted_iota(jnp.int32, shape, dim)


def ring(extent, step):
    return min(step, extent - step)


def pool_offsets(dims):
    ny, nx, nc = dims
    steps = [(a, b, c) for a in range(ny) for b in range(nx) for c in range(nc)][1:]
    return sorted(steps, key=lambda s: -(ring(ny, s[0]) + ring(nx, s[1])) * 2 - s[2])


def pool_partner(me, dims, step):
    ny, nx, nc = dims
    y = lax.rem(me // (nx * nc) + step[0], ny)
    x = lax.rem(lax.rem(me // nc, nx) + step[1], nx)
    c = lax.rem(lax.rem(me, nc) + step[2], nc)
    return (y * nx + x) * nc + c


def wait_bytes(ref, sem):
    pltpu.make_async_copy(ref, ref, sem).wait()


def kernel(
    dims,
    heads,
    hid_hbm,
    q_hbm,
    w_hbm,
    down_hbm,
    up_hbm,
    pages_hbm,
    rai_hbm,
    app_hbm,
    table_hbm,
    length_hbm,
    new_kv_ref,
    attended_ref,
    hid,
    q,
    w,
    down,
    up,
    pages,
    rai,
    app,
    table,
    length,
    send_rows,
    recv_rows,
    send_meta,
    recv_meta,
    row_f32,
    send_base,
    recv_base,
    send_rank,
    recv_rank,
    up_mask,
    send_delta,
    recv_delta,
    bias,
    scores,
    load_sem,
    row_sems,
    meta_sems,
    base_sems,
    rank_sems,
    delta_sems,
    up_sems,
):
    me = lax.axis_index("pool")
    tp = lax.axis_index("tp")
    n_pool = dims[0] * dims[1] * dims[2]
    n_tp = heads
    rows, feats = hid.shape
    chunks = feats // LANES
    adapters = down.shape[0] // feats
    head = LANES
    group = q.shape[1] // head
    slots = CAP * n_pool
    span = CAP * chunks
    offsets = pool_offsets(dims)
    partners = [pool_partner(me, dims, s) for s in offsets]
    core = lax.rem(me, 2)
    chip = me // 2
    other_core = me + 1 - 2 * core
    gather = me + 1 - core
    n_chips = n_pool // 2
    chip_slots = 2 * CAP
    tp_steps = sorted(range(1, n_tp), key=lambda s: -ring(n_tp, s))
    tp_partners = [lax.rem(tp + s, n_tp) for s in tp_steps]

    loads = [
        pltpu.make_async_copy(src, dst, load_sem.at[i])
        for i, (src, dst) in enumerate(
            (
                (rai_hbm, rai),
                (app_hbm, app),
                (hid_hbm, hid),
                (w_hbm, w),
                (table_hbm, table),
                (length_hbm, length),
                (q_hbm, q),
                (down_hbm, down),
                (pages_hbm, pages),
                (up_hbm, up.at[pl.ds(adapters * LANES, adapters * LANES)]),
            )
        )
    ]
    (l_rai, l_app, l_hid, l_w, l_table, l_length, l_q, l_down, l_pages, l_up) = loads
    barrier = pltpu.get_barrier_semaphore()
    for t in tp_partners:
        pl.semaphore_signal(barrier, inc=1, device_id=(me, t), device_id_type=MESH)
        pl.semaphore_signal(barrier, inc=1, device_id=(other_core, t), device_id_type=MESH)
    for p in partners:
        pl.semaphore_signal(barrier, inc=1, device_id=(p, tp), device_id_type=MESH)
    for load in loads:
        load.start()

    l_rai.wait()
    l_app.wait()
    eye = iota((rows, rows), 0) == iota((rows, rows), 1)
    rai_row = rai[...].astype(F32)
    rai_col = jnp.sum(jnp.where(eye, rai_row, 0.0), axis=1, keepdims=True)
    n_adapters = app.shape[1]
    hit = rai_col == iota((rows, n_adapters), 1).astype(F32)
    position = jnp.sum(jnp.where(hit, app[...].astype(F32), 0.0), axis=1, keepdims=True)
    owner = jnp.floor(position * (1.0 / adapters))
    local = position - owner * adapters
    owner_row = jnp.sum(jnp.where(eye, owner, 0.0), axis=0, keepdims=True)
    earlier = iota((rows, rows), 1) < iota((rows, rows), 0)
    rank = jnp.sum(jnp.where((owner == owner_row) & earlier, 1.0, 0.0), axis=1, keepdims=True)
    target = owner * CAP + rank

    lanes = chunks * rows
    lane_eye = iota((rows, lanes), 0) == lax.rem(iota((rows, lanes), 1), rows)
    target_lane = jnp.sum(jnp.where(lane_eye, target, 0.0), axis=0, keepdims=True)
    line = iota((slots * chunks, lanes), 0)
    place = ((line // chunks).astype(F32) == target_lane) & (
        lax.rem(line, chunks) == iota((slots * chunks, lanes), 1) // rows
    )
    place = jnp.where(place, 1.0, 0.0).astype(BF16)
    l_hid.wait()
    stacked = jnp.concatenate([hid[:, c * LANES : (c + 1) * LANES] for c in range(chunks)], axis=0)
    packets = jnp.dot(place, stacked, preferred_element_type=F32).astype(BF16)
    send_rows[...] = packets.reshape(n_pool, span, LANES)
    wide_rows = chip_slots * rows
    held_by = iota((n_chips, wide_rows), 0) * chip_slots + iota((n_chips, wide_rows), 1) // rows
    held_by = jnp.where(held_by.astype(F32) == target_lane[:, :wide_rows], 1.0, 0.0).astype(BF16)
    quarter = iota((rows, LANES), 1) // (LANES // chip_slots)
    lines = jnp.concatenate([jnp.where(quarter == n, local, 0.0) for n in range(chip_slots)], axis=0)
    send_meta[...] = jnp.dot(
        held_by, lines.astype(BF16), preferred_element_type=F32
    ).reshape(n_chips, 1, LANES)

    pl.semaphore_wait(barrier, len(partners) + 2 * len(tp_partners))

    for p in partners:
        pltpu.make_async_remote_copy(
            src_ref=send_rows.at[p],
            dst_ref=recv_rows.at[me],
            send_sem=row_sems.at[0],
            recv_sem=row_sems.at[1],
            device_id=(p, tp),
            device_id_type=MESH,
        ).start()
        pltpu.make_async_remote_copy(
            src_ref=send_meta.at[p // 2],
            dst_ref=recv_meta.at[me],
            send_sem=meta_sems.at[0],
            recv_sem=meta_sems.at[1],
            device_id=(p, tp),
            device_id_type=MESH,
        ).start()
    recv_rows[me] = send_rows[me]
    recv_meta[me] = send_meta[chip]
    up_half = adapters * LANES
    up_copy = pltpu.make_async_remote_copy(
        src_ref=up_hbm,
        dst_ref=up.at[pl.ds(0, up_half)],
        send_sem=up_sems.at[0],
        recv_sem=up_sems.at[1],
        device_id=(other_core, tp),
        device_id_type=MESH,
    )

    @pl.when(core == 0)
    def _():
        up_copy.start()

    wide = LANES * heads
    spread = iota((LANES, wide), 0) == iota((LANES, wide), 1) // heads
    spread = jnp.where(spread, 1.0, 0.0).astype(BF16)
    repeated = jnp.dot(stacked, spread, preferred_element_type=F32).astype(BF16)
    head_of_lane = lax.rem(iota((rows, wide), 1), heads)
    l_w.wait()
    base = jnp.zeros((heads * rows, 2 * head), F32)
    for c in range(chunks):
        piece = repeated[c * rows : (c + 1) * rows, :]
        masked = jnp.concatenate(
            [jnp.where(head_of_lane == g, piece, jnp.zeros_like(piece)) for g in range(heads)], axis=0
        )
        base += jnp.dot(masked, w[c * wide : (c + 1) * wide, :], preferred_element_type=F32)
    send_base[...] = base.astype(BF16).reshape(heads, rows, 2 * head)
    for t in tp_partners:
        pltpu.make_async_remote_copy(
            src_ref=send_base.at[t],
            dst_ref=recv_base.at[tp],
            send_sem=base_sems.at[0],
            recv_sem=base_sems.at[1],
            device_id=(me, t),
            device_id_type=MESH,
        ).start()
    recv_base[tp] = send_base[tp]

    l_down.wait()
    others = pl.ds(0, n_pool - 1)
    wait_bytes(recv_rows.at[others], row_sems.at[1])
    wait_bytes(recv_meta.at[others], meta_sems.at[1])
    row_f32[...] = recv_rows[...].astype(F32).reshape(n_pool * span, LANES)
    taken = jnp.concatenate(
        [
            jnp.concatenate(
                [row_f32[pl.ds(s * chunks + c, n_pool, stride=span), :] for c in range(chunks)], axis=1
            )
            for s in range(CAP)
        ],
        axis=0,
    ).astype(BF16)
    meta = recv_meta[...].reshape(n_pool, LANES).astype(BF16)
    apart = iota((LANES, chip_slots * LANES), 1) // LANES * (LANES // chip_slots)
    apart = jnp.where(iota((LANES, chip_slots * LANES), 0) == apart, 1.0, 0.0).astype(BF16)
    spread_meta = jnp.dot(meta, apart, preferred_element_type=F32)
    adapters_of = [
        jnp.concatenate(
            [spread_meta[:, (n * CAP + m) * LANES : (n * CAP + m + 1) * LANES] for m in range(CAP)], axis=0
        )
        for n in range(2)
    ]
    is_one = core.astype(F32)
    adapter_of = adapters_of[0] * (1.0 - is_one) + adapters_of[1] * is_one
    partial = jnp.zeros((slots, LANES), F32)
    for a in range(0, adapters, 2):
        both = jnp.concatenate(
            [down[a * feats : (a + 1) * feats, :], down[(a + 1) * feats : (a + 2) * feats, :]], axis=1
        )
        product = jnp.dot(taken, both, preferred_element_type=F32)
        partial = jnp.where(adapter_of == float(a), product[:, :LANES], partial)
        partial = jnp.where(adapter_of == float(a + 1), product[:, LANES:], partial)
    send_rank[...] = partial.astype(BF16)
    rank_copies = [
        pltpu.make_async_remote_copy(
            src_ref=send_rank,
            dst_ref=recv_rank.at[core * n_tp + tp],
            send_sem=rank_sems.at[0],
            recv_sem=rank_sems.at[1 + core],
            device_id=(gather, t),
            device_id_type=MESH,
        )
        for t in [*tp_partners, tp]
    ]
    for copy in rank_copies[:-1]:
        copy.start()

    @pl.when(core == 0)
    def _():
        rank_copies[-1].start()

    @pl.when(core == 1)
    def _():
        recv_rank[n_tp + tp] = send_rank[...]

    l_table.wait()
    l_length.wait()
    entries, _ = table.shape
    positions = pages.shape[0]
    page = 16
    eye_bf16 = jnp.where(eye, 1.0, 0.0).astype(BF16)
    entry = table[...]
    high, low = entry // 16, lax.rem(entry, 16)
    turn = (((1,), (1,)), ((), ()))
    table_rows = (
        lax.dot_general(eye_bf16, high.astype(F32).astype(BF16), turn, preferred_element_type=F32) * 16.0
        + lax.dot_general(eye_bf16, low.astype(F32).astype(BF16), turn, preferred_element_type=F32)
    )
    length_col = jnp.sum(jnp.where(eye, length[...].astype(F32), 0.0), axis=1, keepdims=True)
    page_blocks = pl.cdiv(positions // page, LANES)
    page_id = iota((rows, page_blocks * LANES), 1).astype(F32)
    held = jnp.zeros((rows, page_blocks * LANES), F32)
    for j in range(entries):
        valid = jnp.clip(length_col - float(page * j), 0.0, float(page))
        held += jnp.where(table_rows[:, j : j + 1] == page_id, valid, 0.0)
    held = held.astype(BF16)
    widen = iota((LANES, LANES * page), 0) == iota((LANES, LANES * page), 1) // page
    widen = jnp.where(widen, 1.0, 0.0).astype(BF16)
    for b in range(page_blocks):
        first = b * LANES * page
        width = min(LANES * page, positions - first)
        count = jnp.dot(held[:, b * LANES : (b + 1) * LANES], widen[:, :width], preferred_element_type=F32)
        within = lax.rem(iota((rows, width), 1), page).astype(F32)
        bias[:, first : first + width] = jnp.where(within < count, 0.0, NEG)

    l_q.wait()
    l_pages.wait()
    query = jnp.concatenate([q[:, h * head : (h + 1) * head] for h in range(group)], axis=0)
    scale = math.log2(math.e) / math.sqrt(head)
    tile = 256
    tiles = positions // tile
    pairs = group * rows

    def score_step(j, largest):
        at = pl.ds(pl.multiple_of(j * tile, tile), tile)
        s = lax.dot_general(query, pages[at, 0:head], turn, preferred_element_type=F32) * scale
        s = (s.reshape(group, rows, tile) + bias[:, at][None]).reshape(pairs, tile)
        scores[j] = s
        return jnp.maximum(largest, jnp.maximum(s[:, :LANES], s[:, LANES:]))

    largest = lax.fori_loop(0, tiles, score_step, jnp.full((pairs, LANES), NEG, F32))
    largest = jnp.max(largest, axis=1, keepdims=True)

    def weight_step(j, carry):
        total, blended = carry
        at = pl.ds(pl.multiple_of(j * tile, tile), tile)
        weight = jnp.exp2(scores[j] - largest)
        total = total + weight[:, :LANES] + weight[:, LANES:]
        blended = blended + jnp.dot(
            weight.astype(BF16), pages[at, head : 2 * head], preferred_element_type=F32
        )
        return total, blended

    wait_bytes(recv_rows.at[others], row_sems.at[0])
    wait_bytes(recv_meta.at[others], meta_sems.at[0])
    wait_bytes(recv_base.at[pl.ds(0, n_tp - 1)], base_sems.at[0])
    l_up.wait()

    @pl.when(core == 1)
    def _():
        key_lane = iota((slots, LANES), 1) < LANES // 2
        rank_width = LANES // 2
        for n in range(2):
            for a in range(0, adapters, 2):
                on = jnp.where(key_lane, adapters_of[n], adapters_of[n] - 1.0) == float(a)
                up_mask[n * slots : (n + 1) * slots, a * rank_width : (a + 2) * rank_width] = jnp.where(
                    on, 1.0, 0.0
                ).astype(BF16)
        wait_bytes(up.at[pl.ds(0, up_half)], up_sems.at[1])
        for n in (1, 0):
            first = n * n_tp
            wait_bytes(recv_rank.at[pl.ds(first, n_tp - n)], rank_sems.at[1 + n])
            shrink = recv_rank[first].astype(F32)
            for t in range(1, n_tp):
                shrink += recv_rank[first + t].astype(F32)
            shrink = shrink.astype(BF16).astype(F32)
            swapped = pltpu.roll(shrink, rank_width, 1)
            mask = up_mask[n * slots : (n + 1) * slots, :]
            spread_rank = jnp.concatenate(
                [
                    jnp.concatenate([twice.astype(BF16)] * (adapters // 2), axis=1) * mask
                    for twice in (
                        jnp.where(key_lane, shrink, swapped),
                        jnp.where(key_lane, swapped, shrink),
                    )
                ],
                axis=0,
            )
            maps = jnp.concatenate(
                [
                    jnp.concatenate(
                        [
                            up[pl.ds(n * up_half + a * LANES + half * rank_width, rank_width), :]
                            for a in range(adapters)
                        ],
                        axis=0,
                    )
                    for half in range(2)
                ],
                axis=1,
            )
            both = jnp.dot(spread_rank, maps, preferred_element_type=F32)
            for half in range(2):
                delta = both[half * slots : (half + 1) * slots, half * LANES : (half + 1) * LANES]
                delta = (delta * adapter_scale).astype(BF16).astype(F32)
                for m in range(CAP):
                    line = (n * CAP + m) * 2 + half
                    send_delta[pl.ds(line, n_pool, stride=2 * chip_slots), :] = delta[
                        m * n_pool : (m + 1) * n_pool, :
                    ]
        packet = 2 * chip_slots
        here = pl.ds(pl.multiple_of(chip * packet, packet), packet)
        for p in partners:
            pltpu.make_async_remote_copy(
                src_ref=send_delta.at[pl.ds(pl.multiple_of(p * packet, packet), packet)],
                dst_ref=recv_delta.at[here],
                send_sem=delta_sems.at[0],
                recv_sem=delta_sems.at[1],
                device_id=(p, tp),
                device_id_type=MESH,
            ).start()
        recv_delta[here, :] = send_delta[pl.ds(pl.multiple_of(me * packet, packet), packet), :]

    zero = jnp.zeros((pairs, LANES), F32)
    total, blended = lax.fori_loop(0, tiles, weight_step, (zero, zero))
    total = jnp.sum(total, axis=1, keepdims=True)

    wait_bytes(recv_base.at[pl.ds(0, n_tp - 1)], base_sems.at[1])
    base = recv_base[0].astype(F32)
    for t in range(1, n_tp):
        base += recv_base[t].astype(F32)
    column = iota((rows, 2 * slots), 1)
    mine = (column // 2).astype(F32) == target
    picks = [mine & (lax.rem(column, 2) == half) for half in range(2)]
    pick = jnp.concatenate([jnp.where(m, 1.0, 0.0) for m in picks], axis=0).astype(BF16)
    packet = 2 * chip_slots

    @pl.when(core == 0)
    def _():
        wait_bytes(up.at[pl.ds(0, up_half)], up_sems.at[0])
        wait_bytes(recv_rank.at[pl.ds(0, n_tp)], rank_sems.at[0])
        wait_bytes(recv_delta, delta_sems.at[1])

    @pl.when(core == 1)
    def _():
        wait_bytes(recv_rank.at[pl.ds(0, n_tp - 1)], rank_sems.at[0])
        wait_bytes(recv_delta.at[pl.ds(0, (n_chips - 1) * packet)], delta_sems.at[1])

    arrived = recv_delta[...].astype(BF16)
    rows_delta = jnp.dot(pick, arrived, preferred_element_type=F32)
    new_key = (base[:, :head] + rows_delta[:rows]).astype(BF16)
    new_value = (base[:, head:] + rows_delta[rows:]).astype(BF16)
    new_kv_ref[:, :head] = new_key
    new_kv_ref[:, head:] = new_value
    new_key, new_value = new_key.astype(F32)[None], new_value.astype(F32)[None]
    own = jnp.sum(
        (query.astype(F32).reshape(group, rows, head) * new_key).reshape(pairs, head), axis=1, keepdims=True
    ) * scale
    top = jnp.maximum(largest, own)
    fade = jnp.exp2(largest - top)
    own = jnp.exp2(own - top)
    total = total * fade + own
    rounded = own.astype(BF16).astype(F32)
    spread_own = jnp.broadcast_to(rounded, (pairs, head)).reshape(group, rows, head) * new_value
    result = (blended * fade + spread_own.reshape(pairs, head)) * (1.0 / total)
    for h in range(group):
        attended_ref[:, h * head : (h + 1) * head] = result[h * rows : (h + 1) * rows].astype(BF16)

    @pl.when(core == 1)
    def _():
        wait_bytes(send_delta.at[pl.ds(0, (n_pool - 1) * packet)], delta_sems.at[0])


def emit(new_kv_in, attended_in, new_kv_out, attended_out, sem):
    copies = [
        pltpu.make_async_copy(attended_in, attended_out, sem.at[0]),
        pltpu.make_async_copy(new_kv_in, new_kv_out, sem.at[1]),
    ]
    for copy in copies:
        copy.start()
    for copy in copies:
        copy.wait()


def body(
    dims,
    hidden,
    queries,
    key_value_weight,
    adapter_down_maps,
    adapter_up_maps,
    key_value_pages,
    row_adapter_index,
    adapter_page_position,
    row_page_table,
    cached_length,
):
    rows, feats = hidden.shape
    heads = key_value_weight.shape[1]
    width = key_value_weight.shape[2]
    adapters, _, double_rank = adapter_down_maps.shape
    n_pages, page = key_value_pages.shape[:2]
    n_pool = dims[0] * dims[1] * dims[2]
    positions = n_pages * page
    slots = CAP * n_pool
    span = CAP * feats // LANES
    pairs = rows * queries.shape[1] // LANES
    operands = (
        hidden,
        queries,
        key_value_weight.reshape(feats * heads, width),
        adapter_down_maps.reshape(adapters * feats, double_rank),
        adapter_up_maps.reshape(adapters * double_rank, width // 2),
        key_value_pages.reshape(positions, width),
        row_adapter_index.reshape(1, rows),
        adapter_page_position.reshape(1, -1),
        row_page_table.T,
        cached_length.reshape(1, rows),
    )
    vmem = [pltpu.VMEM(x.shape, x.dtype) for x in operands]
    vmem[4] = pltpu.VMEM((2 * adapters * double_rank, width // 2), BF16)
    scratch = vmem + [
        pltpu.VMEM((n_pool, span, LANES), BF16),
        pltpu.VMEM((n_pool, span, LANES), BF16),
        pltpu.VMEM((n_pool // 2, 1, LANES), F32),
        pltpu.VMEM((n_pool, 1, LANES), F32),
        pltpu.VMEM((n_pool * span, LANES), F32),
        pltpu.VMEM((heads, rows, width), BF16),
        pltpu.VMEM((heads, rows, width), BF16),
        pltpu.VMEM((slots, LANES), BF16),
        pltpu.VMEM((2 * heads, slots, LANES), BF16),
        pltpu.VMEM((2 * slots, adapters * LANES // 2), BF16),
        pltpu.VMEM((4 * slots, LANES), F32),
        pltpu.VMEM((2 * slots, LANES), F32),
        pltpu.VMEM((rows, positions), F32),
        pltpu.VMEM((positions // 256, pairs, 256), F32),
        pltpu.SemaphoreType.DMA((len(operands),)),
        *[pltpu.SemaphoreType.DMA((3,)) for _ in range(6)],
    ]
    new_kv, attended = pl.pallas_call(
        functools.partial(kernel, dims, heads),
        out_shape=(
            pltpu.VMEM((rows, width), BF16),
            pltpu.VMEM(queries.shape, BF16),
        ),
        in_specs=[pl.BlockSpec(memory_space=pl.ANY)] * len(operands),
        out_specs=(pl.BlockSpec(memory_space=pltpu.VMEM),) * 2,
        scratch_shapes=scratch,
        compiler_params=pltpu.CompilerParams(
            collective_id=0, has_side_effects=True, vmem_limit_bytes=60 * 1024 * 1024
        ),
        name="decode_step",
    )(*operands)
    new_kv, attended = pl.pallas_call(
        emit,
        out_shape=(
            jax.ShapeDtypeStruct(new_kv.shape, BF16),
            jax.ShapeDtypeStruct(attended.shape, BF16),
        ),
        in_specs=[pl.BlockSpec(memory_space=pl.ANY)] * 2,
        out_specs=(pl.BlockSpec(memory_space=pl.ANY),) * 2,
        scratch_shapes=[pltpu.SemaphoreType.DMA((2,))],
        compiler_params=pltpu.CompilerParams(vmem_limit_bytes=1024 * 1024),
        name="emit",
    )(new_kv, attended)
    return new_kv.reshape(rows, 1, width), attended


def solution(mesh):
    placed = (
        P("pool", "tp"),
        P("pool", "tp"),
        P("tp", None, None),
        P("pool", "tp", None),
        P("pool", None, None, "tp", None),
        P("pool", None, "tp", None),
        P("pool"),
        P(),
        P("pool", None),
        P("pool"),
    )
    n_pool = mesh.shape["pool"]
    dims = (4, 4, 2) if n_pool == 32 else (1, n_pool // 2, 2)
    return jax.shard_map(
        functools.partial(body, dims),
        mesh=mesh,
        in_specs=placed,
        out_specs=(P("pool", "tp", None), P("pool", "tp")),
        check_vma=False,
    )
```
